1024 devices in a mesh: tens: 64 (over x, z), tile: 16 (over y, core).
Axes of the slice: x: 4, y: 8, z: 16, core: 2. Of those that a mesh axis runs over, the one named last changes fastest.
Arguments:
- integrals: bfloat16 [4096, 8192], P('tens', 'tile'), may hold values from -1 to 1
- occ_blocks: bfloat16 [64, 64, 256], replicated, may hold values from -0.375 to 0.375
- virt_blocks: bfloat16 [64, 64, 256], replicated, may hold values from -0.375 to 0.375
- occ_partners: int32 [64, 4], replicated, may hold values from 0 to 63
- virt_partners: int32 [64, 4], replicated, may hold values from 0 to 63
- occ_counts: int32 [64], replicated, may hold values from 1 to 4, as said below
- virt_counts: int32 [64], replicated, may hold values from 1 to 4, as said below
Outputs:
- chi_tiles: float32 [8192, 64, 128], P('tile', 'tens')
The draws below stay inside these ranges and needn't reach their ends.
Inputs may be any that keep to these rules, and one draw needn't show every extreme that they name: `occ_counts`: every draw has one or more pair blocks with all 4 slots in use. `virt_counts`: every draw has one or more pair blocks with all 4 slots in use.
All inputs are finite; a program needn't handle non-finite values.
Results may differ from the reference program's by a relative error of at most 0.0041.
Values may be sent and summed in bfloat16 or wider, within the bound.
No kernel may reach another device: no remote copies, remote signals or barrier semaphores. Data moves between devices by JAX's collectives and lax.ppermute only.
A program may use at most 128 MiB of HBM per device.

```python
import jax
import jax.numpy as jnp

RI = 8192
BLK = 64
NNZ = 4
NPB = 64
PAIRS = 4096
QJ = 8
N_TENS = 64
N_TILE = 16


def counts_law(key):
    first, second = jax.random.split(key)
    counts = jax.random.randint(first, (NPB,), 1, NNZ + 1)
    chosen = jax.random.randint(second, (), 0, NPB)
    return jnp.where(jnp.arange(NPB) == chosen, NNZ, counts).astype(jnp.int32)


def draw_occ_counts(key, part):
    key = jax.random.fold_in(key, 11)
    return counts_law(key)


def draw_virt_counts(key, part):
    key = jax.random.fold_in(key, 23)
    return counts_law(key)


def set_ends(values, own_key, low, high):
    longest = values.shape.index(max(values.shape))
    spots = []
    for shift in (0, 1):
        where = [jax.random.randint(jax.random.fold_in(own_key, axis), (), 0, length) for axis, length in enumerate(values.shape)]
        where[longest] = (where[longest] + shift) % values.shape[longest]
        spots.append(tuple(where))
    return values.at[spots[0]].set(low).at[spots[1]].set(high)


def level_of(key, shape, cuts, least, top_value):
    def one(axis_at, parts):
        steps = jax.random.uniform(jax.random.fold_in(jax.random.fold_in(key, 6), axis_at), (parts,), jnp.float32, least / len(cuts), top_value / len(cuts))
        return jnp.repeat(jnp.exp(steps), shape[axis_at] // parts).reshape((-1,) + (1,) * (len(shape) - axis_at - 1))

    factor_of = one(*cuts[0])
    for cut in cuts[1:]:
        factor_of = factor_of * one(*cut)
    return factor_of


def gaussian(key, shape, scale, reach, pieces=(), kind=jnp.bfloat16):
    gain = level_of(key, shape, pieces, -0.22, 0.18) if pieces else 1.0
    drawn = jax.random.normal(key, shape, jnp.float32) * scale * gain
    return jnp.minimum(jnp.maximum(drawn, -reach), reach).astype(kind)


def setup_inputs(seed: int = 0) -> dict:
    streams_of = jax.random.split(jax.random.key(seed), 8)
    integrals = gaussian(streams_of[0], (PAIRS, RI), 0.125, 1.0, ((0, 64), (1, 16)))
    occ_blocks = gaussian(streams_of[1], (NPB, BLK, NNZ * BLK), (BLK * NNZ) ** -0.5, 0.375)
    virt_blocks = gaussian(streams_of[2], (NPB, BLK, NNZ * BLK), (BLK * NNZ) ** -0.5, 0.375)
    occ_partners = set_ends(jax.random.randint(streams_of[3], (NPB, NNZ), 0, NPB), jax.random.fold_in(streams_of[3], 1), 0, NPB - 1).astype(jnp.int32)
    virt_partners = set_ends(jax.random.randint(streams_of[4], (NPB, NNZ), 0, NPB), jax.random.fold_in(streams_of[4], 1), 0, NPB - 1).astype(jnp.int32)
    occ_counts = draw_occ_counts(jax.random.fold_in(streams_of[7], 71), 0)
    virt_counts = draw_virt_counts(jax.random.fold_in(streams_of[7], 71), 0)
    return {"integrals": integrals, "occ_blocks": occ_blocks, "virt_blocks": virt_blocks, "occ_partners": occ_partners, "virt_partners": virt_partners, "occ_counts": occ_counts, "virt_counts": virt_counts}


def pair_mix(source, partners, counts, blocks):
    block_count = partners.shape[0]
    block_rows = blocks.shape[1]
    grouped = source.reshape(block_count, block_rows, source.shape[1])
    summed = jnp.zeros(grouped.shape, jnp.float32)
    for neighbour in range(partners.shape[1]):
        active = (counts > neighbour).astype(blocks.dtype)
        weights = blocks[:, :, neighbour * block_rows:(neighbour + 1) * block_rows] * active[:, None, None]
        chosen = jnp.take(grouped, partners[:, neighbour], axis=0)
        summed = summed + jnp.einsum("kij,kjp->kip", weights.astype(jnp.float32), chosen.astype(jnp.float32))
    return summed.reshape(source.shape).astype(jnp.bfloat16)


def reference(integrals, occ_blocks, virt_blocks, occ_partners, virt_partners, occ_counts, virt_counts):
    occ_mixed = pair_mix(integrals, occ_partners, occ_counts, occ_blocks)
    virt_mixed = pair_mix(integrals, virt_partners, virt_counts, virt_blocks)
    chi_full = jnp.dot(occ_mixed.T, virt_mixed, preferred_element_type=jnp.float32)
    reordered = chi_full.reshape(RI, N_TILE, N_TENS, QJ).transpose(0, 2, 1, 3)
    return reordered.reshape(RI, N_TENS, N_TILE * QJ)
```

```python
import functools

import jax
import jax.numpy as jnp
from jax import lax
from jax.experimental import pallas as pl
from jax.experimental.pallas import tpu as pltpu
from jax.sharding import Mesh
from jax.sharding import PartitionSpec as P

NX = 4
NC = 2
BLK = 64
NNZ = 4
QJ = 8
LANES = 128
SUB = 16
FOLD = BLK // SUB
WIDE = FOLD * QJ

VMEM = pl.BlockSpec(memory_space=pltpu.VMEM)
SMEM = pl.BlockSpec(memory_space=pltpu.SMEM)
PARAMS = pltpu.CompilerParams(vmem_limit_bytes=48 * 1024 * 1024)


def lane_ids(rows):
    return lax.broadcasted_iota(jnp.int32, (rows, LANES), 1)


def pack_kernel(raw_ref, out_ref):
    parts = []
    for q in range(FOLD):
        for xs in range(NX):
            piece = raw_ref[q * SUB:(q + 1) * SUB, xs * LANES:(xs + 1) * LANES]
            parts.append(piece.astype(jnp.float32))
    lane_block = lane_ids(SUB) // QJ
    for bit in (1, 2, 4, 8):
        high = (lane_block & bit) != 0
        step = bit * QJ
        swapped = list(parts)
        for m in range(len(parts)):
            if m & bit:
                continue
            low_part, high_part = parts[m], parts[m | bit]
            swapped[m] = jnp.where(high, pltpu.roll(high_part, step, 1), low_part)
            swapped[m | bit] = jnp.where(high, high_part, pltpu.roll(low_part, LANES - step, 1))
        parts = swapped
    for z, part in enumerate(parts):
        value = part.astype(jnp.bfloat16)
        for x in range(NX):
            out_ref[x * len(parts) + z] = value


def mix_kernel(
    part_ref, vp_ref, vc_ref, op_ref, oc_ref, cols_ref, vb_ref, ob_ref, out_ref, spread, mixed, total
):
    blocks = cols_ref.shape[0]
    mine = total.shape[0] - 1
    group = lane_ids(SUB) // WIDE
    first = part_ref[0] * mine

    def widen(k, carry):
        value = cols_ref[k].astype(jnp.float32)
        for q in range(FOLD):
            spread[k, q * SUB:(q + 1) * SUB, :] = jnp.where(group == q, value, 0.0).astype(jnp.bfloat16)
        return carry

    lax.fori_loop(0, blocks, widen, 0, unroll=8)
    spread[blocks] = jnp.zeros(spread.shape[1:], spread.dtype)
    total[...] = jnp.zeros_like(total)

    def virt(k, carry):
        count = vc_ref[k]
        chosen = [
            spread[jnp.where(s < count, vp_ref[s, k], blocks)] for s in range(NNZ)
        ]
        summed = jnp.dot(
            vb_ref[k], jnp.concatenate(chosen, axis=0), preferred_element_type=jnp.float32
        )
        turned = summed.T
        folded = turned[:WIDE]
        for q in range(1, FOLD):
            folded = folded + turned[q * WIDE:(q + 1) * WIDE]
        mixed[k] = folded.astype(jnp.bfloat16)
        return carry

    lax.fori_loop(0, blocks, virt, 0, unroll=8)

    def occ(k, carry):
        count = oc_ref[k]
        spreads = jnp.dot(mixed[k], ob_ref[k], preferred_element_type=jnp.float32)
        for s in range(NNZ):
            half = spreads[:, (s // 2) * LANES:(s // 2 + 1) * LANES]
            if s % 2:
                half = pltpu.roll(half, BLK, 1)
            place = op_ref[s, k] - first
            wanted = (s < count) & (place >= 0) & (place < mine)
            place = jnp.where(wanted, place, mine)
            total[place] = total[place] + half
        return carry

    lax.fori_loop(0, blocks, occ, 0, unroll=8)

    low = lane_ids(WIDE) < BLK
    for a in range(0, mine, 2):
        pair = jnp.where(low, total[a], pltpu.roll(total[a + 1], BLK, 1))
        value = pair.astype(jnp.bfloat16)
        for y in range(out_ref.shape[0]):
            out_ref[y, :, a * BLK:(a + 2) * BLK] = value


def dot_kernel(core_ref, own_ref, other_ref, raw_ref, out_ref):
    first = core_ref[0] == 0
    raw = raw_ref[...]
    for y in range(own_ref.shape[0]):
        own = jnp.dot(own_ref[y], raw, preferred_element_type=jnp.float32)
        other = jnp.dot(other_ref[y], raw, preferred_element_type=jnp.float32)
        zero = jnp.where(first, own, other)
        one = jnp.where(first, other, own)
        for xs in range(NX):
            rows = slice(xs * QJ, (xs + 1) * QJ)
            both = jnp.concatenate([zero[rows], one[rows]], axis=0)
            out_ref[xs, y * SUB:(y + 1) * SUB, :] = both.astype(jnp.bfloat16)


def sum_kernel(parts_ref, out_ref):
    summed = parts_ref[0].astype(jnp.float32)
    for part in range(1, parts_ref.shape[0]):
        summed = summed + parts_ref[part].astype(jnp.float32)
    out_ref[...] = summed.T


def call(kernel, out_shape, dtype, specs, flops, scratch=()):
    return pl.pallas_call(
        kernel,
        out_shape=jax.ShapeDtypeStruct(out_shape, dtype),
        in_specs=specs,
        out_specs=VMEM,
        scratch_shapes=list(scratch),
        compiler_params=PARAMS,
        cost_estimate=pl.CostEstimate(flops=flops, bytes_accessed=1 << 20, transcendentals=0),
    )


def on_device(
    nz, ny, integrals, occ_blocks, virt_blocks, occ_partners, virt_partners, occ_counts, virt_counts
):
    blocks = NX * nz
    width = integrals.shape[1]
    rows = nz * BLK
    raw = lax.all_gather(integrals, "z", axis=0, tiled=True)

    packed = call(pack_kernel, (blocks, SUB, LANES), jnp.bfloat16, [VMEM], 1 << 20)(integrals)
    columns = lax.all_to_all(packed, ("x", "z"), 0, 0, tiled=True)
    copies = call(
        mix_kernel,
        (ny, WIDE, rows),
        jnp.bfloat16,
        [SMEM] * 5 + [VMEM] * 3,
        1 << 28,
        [
            pltpu.VMEM((blocks + 1, BLK, LANES), jnp.bfloat16),
            pltpu.VMEM((blocks, WIDE, BLK), jnp.bfloat16),
            pltpu.VMEM((nz + 1, WIDE, LANES), jnp.float32),
        ],
    )(
        lax.axis_index("x").reshape(1),
        virt_partners.T,
        virt_counts,
        occ_partners.T,
        occ_counts,
        columns,
        virt_blocks,
        occ_blocks,
    )
    own = lax.all_to_all(copies, "y", 0, 0, tiled=True)
    other = lax.ppermute(own, "c", [(0, 1), (1, 0)])
    partial = call(
        dot_kernel,
        (NX, ny * NC * QJ, width),
        jnp.bfloat16,
        [SMEM] + [VMEM] * 3,
        1 << 29,
    )(lax.axis_index("c").reshape(1), own, other, raw)
    parts = lax.all_to_all(partial, "x", 0, 0, tiled=True)
    chi_tile = call(sum_kernel, (width, ny * NC * QJ), jnp.float32, [VMEM], 1 << 20)(parts)
    return chi_tile[:, None, :]


def solution(mesh):
    nz = mesh.shape["tens"] // NX
    ny = mesh.shape["tile"] // NC
    fine = Mesh(mesh.devices.reshape(NX, nz, ny, NC), ("x", "z", "y", "c"))
    return jax.shard_map(
        functools.partial(on_device, nz, ny),
        mesh=fine,
        in_specs=(P(("x", "z"), ("y", "c")), P(), P(), P(), P(), P(), P()),
        out_specs=P(("y", "c"), ("x", "z"), None),
        check_vma=False,
    )
```

```python
import functools

import jax
import jax.numpy as jnp
from jax import lax
from jax.experimental import pallas as pl
from jax.experimental.pallas import tpu as pltpu
from jax.sharding import Mesh
from jax.sharding import PartitionSpec as P

NX = 4
NC = 2
BLK = 64
NNZ = 4
QJ = 8
LANES = 128
SUB = 16
WIDE = NX * QJ
LATE = 2
HALF = 2
UNROLL = 4

VMEM = pl.BlockSpec(memory_space=pltpu.VMEM)
SMEM = pl.BlockSpec(memory_space=pltpu.SMEM)
PARAMS = pltpu.CompilerParams(vmem_limit_bytes=16 * 1024 * 1024)


def lane_ids(rows):
    return lax.broadcasted_iota(jnp.int32, (rows, LANES), 1)


def pack_kernel(raw_ref, out_ref):
    turned = []
    for xs in range(HALF):
        pair = [raw_ref[:, at * LANES:(at + 1) * LANES] for at in (xs, xs + HALF)]
        turned.append(jnp.concatenate(pair, axis=0).astype(jnp.float32).T)
    last = raw_ref[BLK - SUB:, :].astype(jnp.float32)[SUB - LATE:]
    tail = [
        last[row:row + 1, at:at + LANES] for row in range(LATE) for at in range(0, raw_ref.shape[1], LANES)
    ]
    parts = out_ref.shape[0] // NX
    for z in range(parts):
        rows = [part[z * QJ:(z + 1) * QJ] for part in turned]
        value = jnp.concatenate(rows + tail, axis=0).astype(jnp.bfloat16)
        for x in range(NX):
            out_ref[x * parts + z] = value


def prep_kernel(
    mine, part_ref, vp_ref, vc_ref, op_ref, oc_ref, vb_ref, ob_ref, turned_ref, near_ref, slots_ref
):
    slot = lax.broadcasted_iota(jnp.int32, vp_ref.shape, 0)
    blocks = vp_ref.shape[1]
    slots_ref[:NNZ, :] = jnp.where(slot < vc_ref[...], vp_ref[...], blocks)
    place = op_ref[...] - part_ref[0] * mine
    wanted = (slot < oc_ref[...]) & (place >= 0) & (place < mine)
    slots_ref[NNZ:, :] = jnp.where(wanted, place, mine)

    def turn(pair, carry):
        both = [vb_ref[2 * pair + n].astype(jnp.float32) for n in range(2)]
        turned_ref[pair] = jnp.concatenate(both, axis=0).T.astype(jnp.bfloat16)
        for n in range(2):
            near_ref[pair, n * BLK:(n + 1) * BLK, :] = ob_ref[2 * pair + n]
        return carry

    lax.fori_loop(0, blocks // 2, turn, 0, unroll=4)


def mix_kernel(
    part_ref, slots_ref, cols_ref, vb_ref, ob_ref, out_ref, late_ref, spread, total
):
    blocks = cols_ref.shape[0]
    mine = total.shape[1] - 1
    first = part_ref[0] * mine
    low_sub = lane_ids(SUB) < BLK
    low = lane_ids(WIDE) < BLK
    row = lax.broadcasted_iota(jnp.int32, (2 * WIDE, LANES), 0)
    kept = (row < WIDE) == (lane_ids(2 * WIDE) < BLK)

    def widen(k, carry):
        value = cols_ref[k, :SUB].astype(jnp.float32)
        swapped = pltpu.roll(value, BLK, 1)
        both = [jnp.where(low_sub, value, swapped), jnp.where(low_sub, swapped, value)]
        spread[k] = jnp.concatenate(both, axis=0).astype(jnp.bfloat16)
        return carry

    lax.fori_loop(0, blocks, widen, 0, unroll=8)
    spread[blocks] = jnp.zeros(spread.shape[1:], spread.dtype)
    total[...] = jnp.zeros_like(total)
    for k in range(mine):
        late_ref[k] = cols_ref[first + k, SUB:]

    def chosen(k):
        reads = [spread[slots_ref[s, k]] for s in range(NNZ)]
        return jnp.concatenate(
            [jnp.where(low, reads[s], reads[s + 1]) for s in range(0, NNZ, 2)], axis=1
        )

    def mix(pair, carry):
        lhs = jnp.concatenate([chosen(2 * pair + n) for n in range(2)], axis=0)
        virt = jnp.dot(lhs, vb_ref[pair], preferred_element_type=jnp.float32)
        virt = jnp.where(kept, virt, 0.0).astype(jnp.bfloat16)
        added = jnp.dot(virt, ob_ref[pair], preferred_element_type=jnp.float32)
        for n in range(2):
            for s in range(NNZ):
                place = slots_ref[NNZ + s, 2 * pair + n]
                at = (s // 2) * LANES
                total[s, place] = total[s, place] + added[n * WIDE:(n + 1) * WIDE, at:at + LANES]
        return carry

    lax.fori_loop(0, blocks // 2, mix, 0, unroll=UNROLL)

    for a in range(0, mine, 2):
        even = [total[0, a + n] + total[2, a + n] for n in range(2)]
        odd = [total[1, a + n] + total[3, a + n] for n in range(2)]
        moved = pltpu.roll(jnp.where(low, even[1], odd[0]), BLK, 1)
        value = (jnp.where(low, even[0], odd[1]) + moved).astype(jnp.bfloat16)
        for y in range(out_ref.shape[0]):
            out_ref[y, :, a * BLK:(a + 2) * BLK] = value


def dot_kernel(mixed_ref, early_ref, late_ref, out_ref, raw_ref):
    pairs, width, rows = mixed_ref.shape
    columns = raw_ref.shape[1]
    for k in range(early_ref.shape[0]):
        tail = late_ref[k].astype(jnp.float32)
        step = columns // LANES
        last = [
            jnp.concatenate([tail[row * step + n:row * step + n + 1] for n in range(step)], axis=1)
            for row in range(LATE)
        ]
        block = jnp.concatenate([early_ref[k].astype(jnp.float32), *last], axis=0)
        raw_ref[k * BLK:(k + 1) * BLK, :] = block.astype(jnp.bfloat16)
    summed = jnp.dot(
        mixed_ref[...].reshape(pairs * width, rows), raw_ref[...], preferred_element_type=jnp.float32
    )
    for pair in range(0, pairs, NC):
        for xs in range(NX):
            both = [
                summed[(pair + c) * width + xs * QJ:(pair + c) * width + (xs + 1) * QJ] for c in range(NC)
            ]
            both = jnp.concatenate(both, axis=0).astype(jnp.bfloat16)
            out_ref[xs, pair * QJ:(pair + NC) * QJ, :] = both


def sum_kernel(parts_ref, out_ref):
    summed = parts_ref[0].astype(jnp.float32)
    for part in range(1, parts_ref.shape[0]):
        summed = summed + parts_ref[part].astype(jnp.float32)
    out_ref[...] = summed.T


def call(kernel, outs, specs, flops, scratch=()):
    shapes = [jax.ShapeDtypeStruct(*out) for out in outs]
    single = len(shapes) == 1
    return pl.pallas_call(
        kernel,
        out_shape=shapes[0] if single else shapes,
        in_specs=specs,
        out_specs=VMEM if single else [VMEM] * len(shapes),
        scratch_shapes=list(scratch),
        compiler_params=PARAMS,
        cost_estimate=pl.CostEstimate(flops=flops, bytes_accessed=1 << 20, transcendentals=0),
    )


def on_device(
    nz, ny, integrals, occ_blocks, virt_blocks, occ_partners, virt_partners, occ_counts, virt_counts
):
    blocks = NX * nz
    width = integrals.shape[1]
    rows = nz * BLK
    bf16 = jnp.bfloat16
    early = BLK - LATE
    chunk = SUB + LATE * width // LANES

    packed = call(pack_kernel, [((blocks, chunk, LANES), bf16)], [VMEM], 1 << 20)(integrals)
    columns = lax.all_to_all(packed, ("x", "z"), 0, 0, tiled=True)
    part = lax.axis_index("x").reshape(1)
    virt_near, occ_near, slots = call(
        functools.partial(prep_kernel, nz),
        [
            ((blocks // 2, NNZ * BLK, 2 * BLK), bf16),
            ((blocks // 2, 2 * BLK, NNZ * BLK), bf16),
            ((2 * NNZ, blocks), jnp.int32),
        ],
        [SMEM] + [VMEM] * 6,
        1 << 28,
    )(
        part,
        virt_partners.T,
        virt_counts[None],
        occ_partners.T,
        occ_counts[None],
        virt_blocks,
        occ_blocks,
    )
    copies, raw_late = call(
        mix_kernel,
        [((ny * NC, WIDE, rows), bf16), ((nz, chunk - SUB, LANES), bf16)],
        [SMEM] * 2 + [VMEM] * 3,
        1 << 28,
        [
            pltpu.VMEM((blocks + 1, WIDE, LANES), bf16),
            pltpu.VMEM((NNZ, nz + 1, WIDE, LANES), jnp.float32),
        ],
    )(part, slots, columns, virt_near, occ_near)
    copies, own_rows = lax.optimization_barrier((copies, integrals[:early]))
    raw_early = lax.all_gather(own_rows, "z", axis=0)
    mixed = lax.all_to_all(copies, ("y", "c"), 0, 0, tiled=True)
    mixed, raw_early = lax.optimization_barrier((mixed, raw_early))
    partial = call(
        dot_kernel,
        [((NX, ny * NC * QJ, width), bf16)],
        [VMEM] * 3,
        1 << 29,
        [pltpu.VMEM((rows, width), bf16)],
    )(mixed, raw_early, raw_late)
    parts = lax.all_to_all(partial, "x", 0, 0, tiled=True)
    chi_tile = call(sum_kernel, [((width, ny * NC * QJ), jnp.float32)], [VMEM], 1 << 20)(parts)
    return chi_tile[:, None, :]


def solution(mesh):
    nz = mesh.shape["tens"] // NX
    ny = mesh.shape["tile"] // NC
    fine = Mesh(mesh.devices.reshape(NX, nz, ny, NC), ("x", "z", "y", "c"))
    return jax.shard_map(
        functools.partial(on_device, nz, ny),
        mesh=fine,
        in_specs=(P(("x", "z"), ("y", "c")), P(), P(), P(), P(), P(), P()),
        out_specs=P(("y", "c"), ("x", "z"), None),
        check_vma=False,
    )
```

```python
import functools

import jax
import jax.numpy as jnp
from jax import lax
from jax.experimental import pallas as pl
from jax.experimental.pallas import tpu as pltpu
from jax.sharding import Mesh
from jax.sharding import PartitionSpec as P

NX = 4
NC = 2
BLK = 64
NNZ = 4
QJ = 8
LANES = 128
SUB = 16
LATE = 2
UNROLL = 16

VMEM = pl.BlockSpec(memory_space=pltpu.VMEM)
SMEM = pl.BlockSpec(memory_space=pltpu.SMEM)
PARAMS = pltpu.CompilerParams(vmem_limit_bytes=16 * 1024 * 1024)


def lane_ids(rows):
    return lax.broadcasted_iota(jnp.int32, (rows, LANES), 1)


def pack_kernel(raw_ref, out_ref):
    last = raw_ref[BLK - SUB:, :].astype(jnp.float32)[SUB - LATE:]
    tail = [
        last[row:row + 1, at:at + LANES] for row in range(LATE) for at in range(0, raw_ref.shape[1], LANES)
    ]
    parts = out_ref.shape[0] // NX
    for x in range(NX):
        piece = raw_ref[:, x * LANES:(x + 1) * LANES]
        turned = jnp.concatenate([piece, piece], axis=0).astype(jnp.float32).T
        for z in range(parts):
            value = jnp.concatenate([turned[z * QJ:(z + 1) * QJ], *tail], axis=0)
            out_ref[x * parts + z] = value.astype(jnp.bfloat16)


def prep_kernel(vp_ref, vc_ref, op_ref, oc_ref, vb_ref, ob_ref, turned_ref, near_ref, slots_ref):
    slot = lax.broadcasted_iota(jnp.int32, vp_ref.shape, 0)
    blocks = vp_ref.shape[1]
    slots_ref[:NNZ, :] = jnp.where(slot < vc_ref[...], vp_ref[...], blocks)
    slots_ref[NNZ:, :] = jnp.where(slot < oc_ref[...], op_ref[...], blocks)

    def turn(pair, carry):
        both = [vb_ref[2 * pair + n].astype(jnp.float32) for n in range(2)]
        turned_ref[pair] = jnp.concatenate(both, axis=0).T.astype(jnp.bfloat16)
        for n in range(2):
            near_ref[pair, n * BLK:(n + 1) * BLK, :] = ob_ref[2 * pair + n]
        return carry

    lax.fori_loop(0, blocks // 2, turn, 0, unroll=4)


def mix_kernel(slots_ref, cols_ref, vb_ref, ob_ref, out_ref, spread, total):
    blocks = cols_ref.shape[0]
    part = out_ref.shape[2] // BLK
    copies = out_ref.shape[0] * part // blocks
    low = lane_ids(SUB) < BLK
    low_out = lane_ids(QJ) < BLK
    row = lax.broadcasted_iota(jnp.int32, (2 * SUB, LANES), 0)
    kept = ((row < SUB) == (lane_ids(2 * SUB) < BLK)) & ((row & (SUB - 1)) < QJ)

    spread[:blocks] = cols_ref[...]
    spread[blocks] = jnp.zeros(spread.shape[1:], spread.dtype)
    total[...] = jnp.zeros_like(total)

    def chosen(k):
        reads = [spread[slots_ref[s, k]] for s in range(NNZ)]
        return jnp.concatenate(
            [jnp.where(low, reads[s], reads[s + 1]) for s in range(0, NNZ, 2)], axis=1
        )

    def mix(pair, carry):
        lhs = jnp.concatenate([chosen(2 * pair + n) for n in range(2)], axis=0)
        virt = jnp.dot(lhs, vb_ref[pair], preferred_element_type=jnp.float32)
        virt = jnp.where(kept, virt, 0.0).astype(jnp.bfloat16)
        added = jnp.dot(virt, ob_ref[pair], preferred_element_type=jnp.float32)
        for n in range(2):
            for s in range(NNZ):
                place = slots_ref[NNZ + s, 2 * pair + n]
                at = (s // 2) * LANES
                total[s, place] = total[s, place] + added[n * SUB:n * SUB + QJ, at:at + LANES]
        return carry

    lax.fori_loop(0, blocks // 2, mix, 0, unroll=UNROLL)

    for a in range(0, blocks, 2):
        even = [total[0, a + n] + total[2, a + n] for n in range(2)]
        odd = [total[1, a + n] + total[3, a + n] for n in range(2)]
        moved = pltpu.roll(jnp.where(low_out, even[1], odd[0]), BLK, 1)
        value = (jnp.where(low_out, even[0], odd[1]) + moved).astype(jnp.bfloat16)
        at = a % part * BLK
        for copy in range(copies):
            out_ref[a // part * copies + copy, :, at:at + LANES] = value


def dot_kernel(part_ref, mixed_ref, early_ref, cols_ref, out_ref, raw_ref):
    part = early_ref.shape[0]
    step = raw_ref.shape[1] // LANES
    for k in range(part):
        tail = cols_ref[part_ref[0] * part + k].astype(jnp.float32)[QJ:]
        last = [
            jnp.concatenate([tail[row * step + n:row * step + n + 1] for n in range(step)], axis=1)
            for row in range(LATE)
        ]
        block = jnp.concatenate([early_ref[k].astype(jnp.float32), *last], axis=0)
        raw_ref[k * BLK:(k + 1) * BLK, :] = block.astype(jnp.bfloat16)
    summed = jnp.dot(mixed_ref[...], raw_ref[...], preferred_element_type=jnp.float32)
    out_ref[...] = summed.astype(jnp.bfloat16)


def sum_kernel(parts_ref, out_ref):
    summed = parts_ref[0].astype(jnp.float32)
    for part in range(1, parts_ref.shape[0]):
        summed = summed + parts_ref[part].astype(jnp.float32)
    out_ref[...] = summed.T


def call(kernel, outs, specs, flops, scratch=()):
    shapes = [jax.ShapeDtypeStruct(*out) for out in outs]
    single = len(shapes) == 1
    return pl.pallas_call(
        kernel,
        out_shape=shapes[0] if single else shapes,
        in_specs=specs,
        out_specs=VMEM if single else [VMEM] * len(shapes),
        scratch_shapes=list(scratch),
        compiler_params=PARAMS,
        cost_estimate=pl.CostEstimate(flops=flops, bytes_accessed=1 << 20, transcendentals=0),
    )


def on_device(
    nz, ny, integrals, occ_blocks, virt_blocks, occ_partners, virt_partners, occ_counts, virt_counts
):
    blocks = NX * nz
    width = integrals.shape[1]
    rows = nz * BLK
    bf16 = jnp.bfloat16
    early = BLK - LATE
    peers = NX * ny * NC

    packed = call(pack_kernel, [((blocks, SUB, LANES), bf16)], [VMEM], 1 << 20)(integrals)
    columns = lax.all_to_all(packed, ("x", "z"), 0, 0, tiled=True)
    virt_near, occ_near, slots = call(
        prep_kernel,
        [
            ((blocks // 2, NNZ * BLK, 2 * BLK), bf16),
            ((blocks // 2, 2 * BLK, NNZ * BLK), bf16),
            ((2 * NNZ, blocks), jnp.int32),
        ],
        [VMEM] * 6,
        1 << 28,
    )(
        virt_partners.T,
        virt_counts[None],
        occ_partners.T,
        occ_counts[None],
        virt_blocks,
        occ_blocks,
    )
    copies = call(
        mix_kernel,
        [((peers, QJ, rows), bf16)],
        [SMEM] + [VMEM] * 3,
        1 << 28,
        [
            pltpu.VMEM((blocks + 1, SUB, LANES), bf16),
            pltpu.VMEM((NNZ, blocks + 1, QJ, LANES), jnp.float32),
        ],
    )(slots, columns, virt_near, occ_near)
    copies, own_rows = lax.optimization_barrier((copies, integrals[:early]))
    raw_early = lax.all_gather(own_rows, "z", axis=0)
    mixed = lax.all_to_all(copies, ("x", "y", "c"), 0, 0, tiled=True)
    mixed, raw_early = lax.optimization_barrier((mixed, raw_early))
    partial = call(
        dot_kernel,
        [((peers * QJ, width), bf16)],
        [SMEM] + [VMEM] * 3,
        1 << 29,
        [pltpu.VMEM((rows, width), bf16)],
    )(lax.axis_index("x").reshape(1), mixed.reshape(peers * QJ, rows), raw_early, columns)
    partial = partial.reshape(NX, ny * NC * QJ, width)
    parts = lax.all_to_all(partial, "x", 0, 0, tiled=True)
    chi_tile = call(sum_kernel, [((width, ny * NC * QJ), jnp.float32)], [VMEM], 1 << 20)(parts)
    return chi_tile[:, None, :]


def solution(mesh):
    nz = mesh.shape["tens"] // NX
    ny = mesh.shape["tile"] // NC
    fine = Mesh(mesh.devices.reshape(NX, nz, ny, NC), ("x", "z", "y", "c"))
    return jax.shard_map(
        functools.partial(on_device, nz, ny),
        mesh=fine,
        in_specs=(P(("x", "z"), ("y", "c")), P(), P(), P(), P(), P(), P()),
        out_specs=P(("y", "c"), ("x", "z"), None),
        check_vma=False,
    )
```

```python
import functools

import jax
import jax.numpy as jnp
from jax import lax
from jax.experimental import pallas as pl
from jax.experimental.pallas import tpu as pltpu
from jax.sharding import Mesh
from jax.sharding import PartitionSpec as P

NX = 4
NC = 2
BLK = 64
NNZ = 4
QJ = 8
LANES = 128
SUB = 16
UNROLL = 16

VMEM = pl.BlockSpec(memory_space=pltpu.VMEM)
SMEM = pl.BlockSpec(memory_space=pltpu.SMEM)
LIMIT = 16 * 1024 * 1024


def lane_ids(rows):
    return lax.broadcasted_iota(jnp.int32, (rows, LANES), 1)


def pack_kernel(raw_ref, out_ref, early_ref):
    early_ref[...] = raw_ref[:early_ref.shape[0], :]
    last = raw_ref[BLK - SUB:, :].astype(jnp.float32)[SUB - 1:]
    pieces = []
    for at in range(0, raw_ref.shape[1], LANES):
        piece = last[:, at:at + LANES]
        pieces += [pltpu.roll(piece, BLK, 1), piece]
    tail = jnp.concatenate(pieces, axis=0)
    low = lane_ids(QJ) < BLK
    parts = out_ref.shape[0] // NX
    for x in range(NX):
        piece = raw_ref[:, x * LANES:(x + 1) * LANES]
        turned = jnp.concatenate([piece, piece], axis=0).astype(jnp.float32).T
        for z in range(parts):
            value = jnp.where(low, turned[z * QJ:(z + 1) * QJ], tail)
            out_ref[x * parts + z] = value.astype(jnp.bfloat16)


def prep_kernel(vp_ref, vc_ref, op_ref, oc_ref, vb_ref, turned_ref, slots_ref):
    slot = lax.broadcasted_iota(jnp.int32, vp_ref.shape, 0)
    blocks = vp_ref.shape[1]
    slots_ref[:NNZ, :] = jnp.where(slot < vc_ref[...], vp_ref[...], blocks)
    slots_ref[NNZ:, :] = jnp.where(slot < oc_ref[...], op_ref[...], blocks)

    def turn(pair, carry):
        both = [vb_ref[2 * pair + n].astype(jnp.float32) for n in range(2)]
        turned_ref[pair] = jnp.concatenate(both, axis=0).T.astype(jnp.bfloat16)
        return carry

    lax.fori_loop(0, blocks // 2, turn, 0, unroll=4)


def virt_kernel(places, cols_ref, vb_ref, mixed_ref, spread):
    blocks = cols_ref.shape[0]
    low = lane_ids(SUB) < BLK
    low_out = lane_ids(QJ) < BLK
    row = lax.broadcasted_iota(jnp.int32, (2 * SUB, LANES), 0)
    kept = ((row < SUB) == (lane_ids(2 * SUB) < BLK)) & ((row & (SUB - 1)) < QJ)

    def widen(k, carry):
        value = cols_ref[k].astype(jnp.float32)
        value = jnp.where(low_out, value, pltpu.roll(value, BLK, 1))
        spread[k] = jnp.concatenate([value, value], axis=0).astype(jnp.bfloat16)
        return carry

    lax.fori_loop(0, blocks, widen, 0, unroll=UNROLL)
    spread[blocks] = jnp.zeros(spread.shape[1:], spread.dtype)

    def chosen(k):
        reads = [spread[places[s, k]] for s in range(NNZ)]
        return jnp.concatenate(
            [jnp.where(low, reads[s], reads[s + 1]) for s in range(0, NNZ, 2)], axis=1
        )

    def virt(pair, carry):
        lhs = jnp.concatenate([chosen(2 * pair + n) for n in range(2)], axis=0)
        both = jnp.dot(lhs, vb_ref[pair], preferred_element_type=jnp.float32)
        mixed_ref[pair] = jnp.where(kept, both, 0.0).astype(jnp.bfloat16)
        return carry

    lax.fori_loop(0, blocks // 2, virt, 0, unroll=UNROLL)


def occ_kernel(places, mixed_ref, ob_ref, out_ref, total):
    blocks = ob_ref.shape[0]
    part = out_ref.shape[2] // BLK
    copies = out_ref.shape[0] * part // blocks
    low_out = lane_ids(QJ) < BLK
    total[...] = jnp.zeros_like(total)

    def occ(pair, carry):
        rhs = jnp.concatenate([ob_ref[2 * pair + n] for n in range(2)], axis=0)
        added = jnp.dot(mixed_ref[pair], rhs, preferred_element_type=jnp.float32)
        for n in range(2):
            for s in range(NNZ):
                place = places[NNZ + s, 2 * pair + n]
                at = (s // 2) * LANES
                total[s, place] = total[s, place] + added[n * SUB:n * SUB + QJ, at:at + LANES]
        return carry

    lax.fori_loop(0, blocks // 2, occ, 0, unroll=UNROLL)

    for a in range(0, blocks, 2):
        even = [total[0, a + n] + total[2, a + n] for n in range(2)]
        odd = [total[1, a + n] + total[3, a + n] for n in range(2)]
        moved = pltpu.roll(jnp.where(low_out, even[1], odd[0]), BLK, 1)
        value = (jnp.where(low_out, even[0], odd[1]) + moved).astype(jnp.bfloat16)
        at = a % part * BLK
        for copy in range(copies):
            out_ref[a // part * copies + copy, :, at:at + LANES] = value


def dot_kernel(part_ref, mixed_ref, early_ref, cols_ref, out_ref, raw_ref):
    part = early_ref.shape[0]
    low = lane_ids(1) < BLK
    for k in range(part):
        tail = cols_ref[part_ref[0] * part + k].astype(jnp.float32)
        last = [
            jnp.where(low, pltpu.roll(tail[2 * n:2 * n + 1], BLK, 1), tail[2 * n + 1:2 * n + 2])
            for n in range(raw_ref.shape[1] // LANES)
        ]
        last = jnp.concatenate(last, axis=1)
        block = jnp.concatenate([early_ref[k].astype(jnp.float32), last], axis=0)
        raw_ref[k * BLK:(k + 1) * BLK, :] = block.astype(jnp.bfloat16)
    summed = jnp.dot(mixed_ref[...], raw_ref[...], preferred_element_type=jnp.float32)
    out_ref[...] = summed.astype(jnp.bfloat16)


def sum_kernel(parts_ref, out_ref):
    summed = parts_ref[0].astype(jnp.float32)
    for part in range(1, parts_ref.shape[0]):
        summed = summed + parts_ref[part].astype(jnp.float32)
    out_ref[...] = summed.T


def call(kernel, outs, specs, flops, scratch=()):
    shapes = [jax.ShapeDtypeStruct(*out) for out in outs]
    single = len(shapes) == 1
    return pl.pallas_call(
        kernel,
        out_shape=shapes[0] if single else shapes,
        in_specs=specs,
        out_specs=VMEM if single else [VMEM] * len(shapes),
        scratch_shapes=list(scratch),
        compiler_params=pltpu.CompilerParams(vmem_limit_bytes=LIMIT),
        cost_estimate=pl.CostEstimate(flops=flops, bytes_accessed=1 << 20, transcendentals=0),
    )


def on_device(
    nz, ny, integrals, occ_blocks, virt_blocks, occ_partners, virt_partners, occ_counts, virt_counts
):
    blocks = NX * nz
    width = integrals.shape[1]
    rows = nz * BLK
    bf16 = jnp.bfloat16
    peers = NX * ny * NC

    packed, early = call(
        pack_kernel, [((blocks, QJ, LANES), bf16), ((BLK - 1, width), bf16)], [VMEM], 1 << 20
    )(integrals)
    columns = lax.all_to_all(packed, ("x", "z"), 0, 0, tiled=True)
    virt_near, slots = call(
        prep_kernel,
        [((blocks // 2, NNZ * BLK, 2 * BLK), bf16), ((2 * NNZ, blocks), jnp.int32)],
        [VMEM] * 5,
        1 << 28,
    )(virt_partners.T, virt_counts[None], occ_partners.T, occ_counts[None], virt_blocks)
    virt = call(
        virt_kernel,
        [((blocks // 2, 2 * SUB, LANES), bf16)],
        [SMEM, VMEM, VMEM],
        1 << 28,
        [pltpu.VMEM((blocks + 1, SUB, LANES), bf16)],
    )(slots, columns, virt_near)
    copies = call(
        occ_kernel,
        [((peers, QJ, rows), bf16)],
        [SMEM, VMEM, VMEM],
        1 << 28,
        [pltpu.VMEM((NNZ, blocks + 1, QJ, LANES), jnp.float32)],
    )(slots, virt, occ_blocks)
    copies, early = lax.optimization_barrier((copies, early))
    raw_early = lax.all_gather(early, "z", axis=0)
    mixed = lax.all_to_all(copies, ("x", "y", "c"), 0, 0, tiled=True)
    mixed, raw_early = lax.optimization_barrier((mixed, raw_early))
    partial = call(
        dot_kernel,
        [((peers * QJ, width), bf16)],
        [SMEM] + [VMEM] * 3,
        1 << 29,
        [pltpu.VMEM((rows, width), bf16)],
    )(lax.axis_index("x").reshape(1), mixed.reshape(peers * QJ, rows), raw_early, columns)
    partial = partial.reshape(NX, ny * NC * QJ, width)
    parts = lax.all_to_all(partial, "x", 0, 0, tiled=True)
    chi_tile = call(sum_kernel, [((width, ny * NC * QJ), jnp.float32)], [VMEM], 1 << 20)(parts)
    return chi_tile[:, None, :]


def solution(mesh):
    nz = mesh.shape["tens"] // NX
    ny = mesh.shape["tile"] // NC
    fine = Mesh(mesh.devices.reshape(NX, nz, ny, NC), ("x", "z", "y", "c"))
    return jax.shard_map(
        functools.partial(on_device, nz, ny),
        mesh=fine,
        in_specs=(P(("x", "z"), ("y", "c")), P(), P(), P(), P(), P(), P()),
        out_specs=P(("y", "c"), ("x", "z"), None),
        check_vma=False,
    )
```

```python
import functools

import jax
import jax.numpy as jnp
from jax import lax
from jax.experimental import pallas as pl
from jax.experimental.pallas import tpu as pltpu
from jax.sharding import Mesh
from jax.sharding import PartitionSpec as P

NX = 4
NC = 2
BLK = 64
NNZ = 4
QJ = 8
LANES = 128
SUB = 16
UNROLL = 32

VMEM = pl.BlockSpec(memory_space=pltpu.VMEM)
SMEM = pl.BlockSpec(memory_space=pltpu.SMEM)
LIMIT = 16 * 1024 * 1024


def lane_ids(rows):
    return lax.broadcasted_iota(jnp.int32, (rows, LANES), 1)


def pack_kernel(raw_ref, out_ref, early_ref):
    early_ref[...] = raw_ref[:early_ref.shape[0], :]
    last = raw_ref[BLK - SUB:, :].astype(jnp.float32)[SUB - 1:]
    pieces = []
    for at in range(0, raw_ref.shape[1], LANES):
        piece = last[:, at:at + LANES]
        pieces += [pltpu.roll(piece, BLK, 1), piece]
    tail = jnp.concatenate(pieces, axis=0)
    low = lane_ids(QJ) < BLK
    parts = out_ref.shape[0] // NX
    for x in range(NX):
        piece = raw_ref[:, x * LANES:(x + 1) * LANES]
        turned = jnp.concatenate([piece, piece], axis=0).astype(jnp.float32).T
        for z in range(parts):
            value = jnp.where(low, turned[z * QJ:(z + 1) * QJ], tail)
            out_ref[x * parts + z] = value.astype(jnp.bfloat16)


def prep_kernel(vp_ref, vc_ref, op_ref, oc_ref, vb_ref, turned_ref, slots_ref):
    slot = lax.broadcasted_iota(jnp.int32, vp_ref.shape, 0)
    blocks = vp_ref.shape[1]
    slots_ref[:NNZ, :] = jnp.where(slot < vc_ref[...], vp_ref[...], blocks)
    slots_ref[NNZ:, :] = jnp.where(slot < oc_ref[...], op_ref[...], blocks)

    def turn(pair, carry):
        both = [vb_ref[2 * pair + n].astype(jnp.float32) for n in range(2)]
        turned_ref[pair] = jnp.concatenate(both, axis=0).T.astype(jnp.bfloat16)
        return carry

    lax.fori_loop(0, blocks // 2, turn, 0, unroll=4)


def virt_kernel(places, cols_ref, vb_ref, mixed_ref, spread):
    blocks = cols_ref.shape[0]
    low = lane_ids(SUB) < BLK
    low_out = lane_ids(QJ) < BLK
    row = lax.broadcasted_iota(jnp.int32, (2 * SUB, LANES), 0)
    kept = ((row < SUB) == (lane_ids(2 * SUB) < BLK)) & ((row & (SUB - 1)) < QJ)

    def widen(k, carry):
        value = cols_ref[k].astype(jnp.float32)
        value = jnp.where(low_out, value, pltpu.roll(value, BLK, 1))
        spread[k] = jnp.concatenate([value, value], axis=0).astype(jnp.bfloat16)
        return carry

    lax.fori_loop(0, blocks, widen, 0, unroll=UNROLL)
    spread[blocks] = jnp.zeros(spread.shape[1:], spread.dtype)

    def chosen(k):
        reads = [spread[places[s, k]] for s in range(NNZ)]
        return jnp.concatenate(
            [jnp.where(low, reads[s], reads[s + 1]) for s in range(0, NNZ, 2)], axis=1
        )

    def virt(pair, carry):
        lhs = jnp.concatenate([chosen(2 * pair + n) for n in range(2)], axis=0)
        both = jnp.dot(lhs, vb_ref[pair], preferred_element_type=jnp.float32)
        mixed_ref[pair] = jnp.where(kept, both, 0.0).astype(jnp.bfloat16)
        return carry

    lax.fori_loop(0, blocks // 2, virt, 0, unroll=UNROLL)


def occ_kernel(places, mixed_ref, ob_ref, out_ref, total):
    blocks = ob_ref.shape[0]
    part = out_ref.shape[2] // BLK
    copies = out_ref.shape[0] * part // blocks
    low_out = lane_ids(QJ) < BLK
    total[...] = jnp.zeros_like(total)

    def occ(pair, carry):
        rhs = jnp.concatenate([ob_ref[2 * pair + n] for n in range(2)], axis=0)
        added = jnp.dot(mixed_ref[pair], rhs, preferred_element_type=jnp.float32)
        for n in range(2):
            for s in range(NNZ):
                place = places[NNZ + s, 2 * pair + n]
                at = (s // 2) * LANES
                total[s, place] = total[s, place] + added[n * SUB:n * SUB + QJ, at:at + LANES]
        return carry

    lax.fori_loop(0, blocks // 2, occ, 0, unroll=UNROLL)

    for a in range(0, blocks, 2):
        even = [total[0, a + n] + total[2, a + n] for n in range(2)]
        odd = [total[1, a + n] + total[3, a + n] for n in range(2)]
        moved = pltpu.roll(jnp.where(low_out, even[1], odd[0]), BLK, 1)
        value = (jnp.where(low_out, even[0], odd[1]) + moved).astype(jnp.bfloat16)
        at = a % part * BLK
        for copy in range(copies):
            out_ref[a // part * copies + copy, :, at:at + LANES] = value


def dot_kernel(part_ref, mixed_ref, early_ref, cols_ref, out_ref, raw_ref):
    part = early_ref.shape[0]
    low = lane_ids(1) < BLK
    for k in range(part):
        tail = cols_ref[part_ref[0] * part + k].astype(jnp.float32)
        last = [
            jnp.where(low, pltpu.roll(tail[2 * n:2 * n + 1], BLK, 1), tail[2 * n + 1:2 * n + 2])
            for n in range(raw_ref.shape[1] // LANES)
        ]
        last = jnp.concatenate(last, axis=1)
        block = jnp.concatenate([early_ref[k].astype(jnp.float32), last], axis=0)
        raw_ref[k * BLK:(k + 1) * BLK, :] = block.astype(jnp.bfloat16)
    summed = jnp.dot(mixed_ref[...], raw_ref[...], preferred_element_type=jnp.float32)
    out_ref[...] = summed.astype(jnp.bfloat16)


def sum_kernel(parts_ref, out_ref):
    summed = parts_ref[0].astype(jnp.float32)
    for part in range(1, parts_ref.shape[0]):
        summed = summed + parts_ref[part].astype(jnp.float32)
    out_ref[...] = summed.T


def call(kernel, outs, specs, flops, scratch=()):
    shapes = [jax.ShapeDtypeStruct(*out) for out in outs]
    single = len(shapes) == 1
    return pl.pallas_call(
        kernel,
        out_shape=shapes[0] if single else shapes,
        in_specs=specs,
        out_specs=VMEM if single else [VMEM] * len(shapes),
        scratch_shapes=list(scratch),
        compiler_params=pltpu.CompilerParams(vmem_limit_bytes=LIMIT),
        cost_estimate=pl.CostEstimate(flops=flops, bytes_accessed=1 << 20, transcendentals=0),
    )


def on_device(
    nz, ny, integrals, occ_blocks, virt_blocks, occ_partners, virt_partners, occ_counts, virt_counts
):
    blocks = NX * nz
    width = integrals.shape[1]
    rows = nz * BLK
    bf16 = jnp.bfloat16
    peers = NX * ny * NC

    packed, early = call(
        pack_kernel, [((blocks, QJ, LANES), bf16), ((BLK - 1, width), bf16)], [VMEM], 1 << 20
    )(integrals)
    columns = lax.all_to_all(packed, ("x", "z"), 0, 0, tiled=True)
    virt_near, slots = call(
        prep_kernel,
        [((blocks // 2, NNZ * BLK, 2 * BLK), bf16), ((2 * NNZ, blocks), jnp.int32)],
        [VMEM] * 5,
        1 << 28,
    )(virt_partners.T, virt_counts[None], occ_partners.T, occ_counts[None], virt_blocks)
    virt = call(
        virt_kernel,
        [((blocks // 2, 2 * SUB, LANES), bf16)],
        [SMEM, VMEM, VMEM],
        1 << 28,
        [pltpu.VMEM((blocks + 1, SUB, LANES), bf16)],
    )(slots, columns, virt_near)
    copies = call(
        occ_kernel,
        [((peers, QJ, rows), bf16)],
        [SMEM, VMEM, VMEM],
        1 << 28,
        [pltpu.VMEM((NNZ, blocks + 1, QJ, LANES), jnp.float32)],
    )(slots, virt, occ_blocks)
    copies, early = lax.optimization_barrier((copies, early))
    raw_early = lax.all_gather(early, "z", axis=0)
    mixed = lax.all_to_all(copies, ("x", "y", "c"), 0, 0, tiled=True)
    mixed, raw_early = lax.optimization_barrier((mixed, raw_early))
    partial = call(
        dot_kernel,
        [((peers * QJ, width), bf16)],
        [SMEM] + [VMEM] * 3,
        1 << 29,
        [pltpu.VMEM((rows, width), bf16)],
    )(lax.axis_index("x").reshape(1), mixed.reshape(peers * QJ, rows), raw_early, columns)
    partial = partial.reshape(NX, ny * NC * QJ, width)
    parts = lax.all_to_all(partial, "x", 0, 0, tiled=True)
    chi_tile = call(sum_kernel, [((width, ny * NC * QJ), jnp.float32)], [VMEM], 1 << 20)(parts)
    return chi_tile[:, None, :]


def solution(mesh):
    nz = mesh.shape["tens"] // NX
    ny = mesh.shape["tile"] // NC
    fine = Mesh(mesh.devices.reshape(NX, nz, ny, NC), ("x", "z", "y", "c"))
    return jax.shard_map(
        functools.partial(on_device, nz, ny),
        mesh=fine,
        in_specs=(P(("x", "z"), ("y", "c")), P(), P(), P(), P(), P(), P()),
        out_specs=P(("y", "c"), ("x", "z"), None),
        check_vma=False,
    )
```
